128 devices in a mesh: row: 16 (over z, x), col: 8 (over y, core).
Axes of the slice: x: 4, y: 4, z: 4, core: 2. Of those that a mesh axis runs over, the one named last changes fastest.
Arguments:
- charges: bfloat16 [65536, 512], P(('row', 'col')), may hold values from -6 to 6
- send_order: int32 [128, 512], P(('row', 'col')), may hold values from 0 to 511, each once within a row
- near_rows: int32 [128, 160], P(('row', 'col')), may hold values from 0 to 15, as said below
- near_cols: int32 [128, 160], P(('row', 'col')), may hold values from 0 to 31, as said below
- near_count: int32 [128], P(('row', 'col')), may hold values from 40 to 160, as said below
- near_blocks: bfloat16 [128, 160, 256, 256], P(('row', 'col')), may hold values from -0.0625 to 0.0625
- far_rows: int32 [128, 64], P(('row', 'col')), may hold values from 0 to 15, as said below
- far_cols: int32 [128, 64], P(('row', 'col')), may hold values from 0 to 31, as said below
- far_count: int32 [128], P(('row', 'col')), may hold values from 32 to 64, as said below
- couplings: bfloat16 [128, 64, 32, 32], P(('row', 'col')), may hold values from -0.25 to 0.25
- row_basis: bfloat16 [256, 32, 256], P('row'), may hold values from -1 to 1
- col_basis: bfloat16 [256, 32, 256], P(('row', 'col')), may hold values from -0.375 to 0.375
Outputs:
- potential: bfloat16 [65536, 512], P(('row', 'col'))
The draws below stay inside these ranges and needn't reach their ends.
Inputs may be any that keep to these rules, and one draw needn't show every extreme that they name: `send_order`: each row j orders the 512 panels of device j once; its places d * 4 to (d + 1) * 4 - 1 are the panels bound for device d. `near_rows`: the live slots of one device name distinct pairs with near_cols, and slots at or beyond the count hold target 0 and column r * 2. On device r * 8 + c, near_cols // 2 differs from r by at most 2. `near_count`: some devices hold the full 160. `far_rows`: every slot of one device names a distinct pair with far_cols. On device r * 8 + c, far_cols // 2 differs from r by more than 2. `far_count`: some device holds the full 64.
All inputs are finite; a program needn't handle non-finite values.
Results may differ from the reference program's by a relative error of at most 0.017.
Values may be sent and summed in bfloat16 or wider, within the bound.
No kernel may reach another device: no remote copies, remote signals or barrier semaphores. Data moves between devices by JAX's collectives and lax.ppermute only.
A program may use at most 128 MiB of HBM per device.

```python
import jax
import jax.numpy as jnp
from jax import lax

B = 256
K = 32
R = 512
CLS = 2
WIN = 2
NEAR_PER = 20
FAR_PER = 8
P_SIZE = 512
PSEG = 4
NCL = 256
N = 65536
NEAR_MOST = 160
FAR_MOST = 64
N_ROW = 16
N_COL = 8
DEVICES = 128


def near_layout(key):
    key = jax.random.fold_in(key, 11)
    device_count = N_ROW * N_COL
    span = (2 * WIN + 1) * CLS
    per_device = N_COL * CLS * span
    keys = jax.random.split(key, device_count + 3)
    orders = jax.vmap(lambda one_key: jax.random.permutation(one_key, per_device))(keys[:device_count]).astype(jnp.int32)
    device_ids = jnp.arange(device_count, dtype=jnp.int32)
    row_ids = device_ids // N_COL
    local_rows = orders // span
    window = orders % span
    slab_rows = row_ids[:, None] - WIN + window // CLS
    outside = ((slab_rows < 0) | (slab_rows >= N_ROW)).astype(jnp.int32)
    ranked = jnp.argsort(outside, axis=1, stable=True)[:, :NEAR_MOST]
    rows_taken = jnp.take_along_axis(local_rows, ranked, axis=1)
    cols_taken = jnp.take_along_axis(slab_rows * CLS + window % CLS, ranked, axis=1)
    usable = per_device - jnp.sum(outside, axis=1)
    counts = jax.random.randint(keys[device_count], (device_count,), NEAR_MOST // 4, NEAR_MOST // 2 + 1)
    heavy_rows = jax.random.randint(keys[device_count + 1], (4,), WIN, N_ROW - WIN)
    heavy_cols = jax.random.randint(keys[device_count + 2], (4,), 0, N_COL)
    counts = counts.at[heavy_rows * N_COL + heavy_cols].set(NEAR_MOST)
    counts = jnp.minimum(counts, usable).astype(jnp.int32)
    live = jnp.arange(NEAR_MOST, dtype=jnp.int32)[None, :] < counts[:, None]
    rows_final = jnp.where(live, rows_taken, 0).astype(jnp.int32)
    cols_final = jnp.where(live, cols_taken, row_ids[:, None] * CLS).astype(jnp.int32)
    return (rows_final, cols_final, counts)


def far_layout(key):
    key = jax.random.fold_in(key, 23)
    device_count = N_ROW * N_COL
    column_set = N_ROW * CLS
    per_device = N_COL * CLS * column_set
    keys = jax.random.split(key, device_count + 2)
    orders = jax.vmap(lambda one_key: jax.random.permutation(one_key, per_device))(keys[:device_count]).astype(jnp.int32)
    device_ids = jnp.arange(device_count, dtype=jnp.int32)
    row_ids = device_ids // N_COL
    local_rows = orders // column_set
    local_cols = orders % column_set
    distance = jnp.abs(local_cols // CLS - row_ids[:, None])
    inside = (distance <= WIN).astype(jnp.int32)
    ranked = jnp.argsort(inside, axis=1, stable=True)[:, :FAR_MOST]
    rows_taken = jnp.take_along_axis(local_rows, ranked, axis=1).astype(jnp.int32)
    cols_taken = jnp.take_along_axis(local_cols, ranked, axis=1).astype(jnp.int32)
    counts = jax.random.randint(keys[device_count], (device_count,), FAR_MOST // 2, FAR_MOST + 1)
    heavy = jax.random.randint(keys[device_count + 1], (1,), 0, device_count)
    counts = counts.at[heavy].set(FAR_MOST).astype(jnp.int32)
    return (rows_taken, cols_taken, counts)


def draw_near_rows(key, part):
    return near_layout(key)[0]


def draw_near_cols(key, part):
    return near_layout(key)[1]


def draw_near_count(key, part):
    return near_layout(key)[2]


def draw_far_rows(key, part):
    return far_layout(key)[0]


def draw_far_cols(key, part):
    return far_layout(key)[1]


def draw_far_count(key, part):
    return far_layout(key)[2]


def levels(key, extent, cuts, least, largest):
    def one(position, shards_of):
        draws = jax.random.uniform(jax.random.fold_in(jax.random.fold_in(key, 6), position), (shards_of,), jnp.float32, least / len(cuts), largest / len(cuts))
        return jnp.repeat(jnp.exp(draws), extent[position] // shards_of).reshape((-1,) + (1,) * (len(extent) - position - 1))

    loudness = one(*cuts[0])
    for cut in cuts[1:]:
        loudness = loudness * one(*cut)
    return loudness


def centred(own_key, shape, width, limit, cuts=(), kind=jnp.bfloat16):
    factor_of = levels(own_key, shape, cuts, -0.22, 0.18) if cuts else 1.0
    drawn = jax.random.normal(own_key, shape, jnp.float32) * width * factor_of
    return jnp.minimum(jnp.maximum(drawn, -limit), limit).astype(kind)


def setup_inputs(seed: int = 0) -> dict:
    splits = jax.random.split(jax.random.key(seed), 13)
    return {
        "charges": centred(splits[0], (N, R), 1.0, 6.0, ((0, 128),)),
        "send_order": jax.vmap(lambda own: jax.random.permutation(own, P_SIZE))(jax.random.split(splits[1], DEVICES)).reshape((DEVICES, P_SIZE)).astype(jnp.int32),
        "near_rows": draw_near_rows(jax.random.fold_in(splits[12], 71), 0),
        "near_cols": draw_near_cols(jax.random.fold_in(splits[12], 71), 0),
        "near_count": draw_near_count(jax.random.fold_in(splits[12], 71), 0),
        "near_blocks": centred(splits[5], (DEVICES, NEAR_MOST, B, B), (B * NEAR_PER * N_COL // 4) ** -0.5, 0.0625, ((0, 128),)),
        "far_rows": draw_far_rows(jax.random.fold_in(splits[12], 71), 0),
        "far_cols": draw_far_cols(jax.random.fold_in(splits[12], 71), 0),
        "far_count": draw_far_count(jax.random.fold_in(splits[12], 71), 0),
        "couplings": centred(splits[9], (DEVICES, FAR_MOST, K, K), (K * FAR_PER * N_COL // 4) ** -0.5, 0.25, ((0, 128),)),
        "row_basis": centred(splits[10], (NCL, K, B), K ** -0.5, 1.0, ((0, 16),)),
        "col_basis": centred(splits[11], (NCL, K, B), B ** -0.5, 0.375, ((0, 128),)),
    }


def reference(charges, send_order, near_rows, near_cols, near_count, near_blocks, far_rows, far_cols, far_count, couplings, row_basis, col_basis):
    device_count = N_ROW * N_COL
    excitations = charges.shape[1]
    span = N_COL * CLS
    source = charges.reshape(device_count, P_SIZE, excitations)
    picked = jnp.take_along_axis(source, send_order[:, :, None].astype(jnp.int32), axis=1)
    tree = picked.reshape(device_count, device_count, PSEG, excitations).transpose(1, 0, 2, 3).reshape(NCL, B, excitations)
    moments = jnp.einsum("gkb,gbr->gkr", col_basis.astype(jnp.float32), tree.astype(jnp.float32)).astype(jnp.bfloat16)
    device_ids = jnp.arange(device_count, dtype=jnp.int32)
    row_ids = device_ids // N_COL
    col_ids = device_ids % N_COL

    def global_cols(local_cols):
        return (((local_cols // CLS) * N_COL + col_ids[:, None]) * CLS + local_cols % CLS).astype(jnp.int32)

    near_live = jnp.arange(NEAR_MOST, dtype=jnp.int32)[None, :] < near_count[:, None]
    far_live = jnp.arange(FAR_MOST, dtype=jnp.int32)[None, :] < far_count[:, None]

    def per_device(total, item):
        blocks, target_near, source_near, live_near, couple, target_far, source_far, live_far, row_id = item
        product = jnp.einsum("sij,sjr->sir", blocks.astype(jnp.float32), tree[source_near].astype(jnp.float32))
        product = jnp.where(live_near[:, None, None], product, jnp.zeros_like(product))
        coupled = jnp.einsum("pkl,plr->pkr", couple.astype(jnp.float32), moments[source_far].astype(jnp.float32))
        coupled = jnp.where(live_far[:, None, None], coupled, jnp.zeros_like(coupled))
        near_local = jnp.zeros((span, B, excitations), jnp.float32).at[target_near].add(product)
        far_local = jnp.zeros((span, K, excitations), jnp.float32).at[target_far].add(coupled)
        first = (row_id * span).astype(jnp.int32)
        basis_slice = lax.dynamic_slice_in_dim(row_basis, first, span, 0)
        expanded = jnp.einsum("gkb,gkr->gbr", basis_slice.astype(jnp.float32), far_local, precision=lax.Precision.HIGHEST)
        term = lax.optimization_barrier((near_local + expanded).astype(jnp.bfloat16)).astype(jnp.float32)
        current = lax.dynamic_slice_in_dim(total, first, span, 0)
        return lax.dynamic_update_slice_in_dim(total, current + term, first, 0), None

    start = jnp.zeros((NCL, B, excitations), jnp.float32)
    items = (near_blocks, near_rows.astype(jnp.int32), global_cols(near_cols), near_live, couplings, far_rows.astype(jnp.int32), global_cols(far_cols), far_live, row_ids)
    total, _ = lax.scan(per_device, start, items)
    return total.reshape(NCL * B, excitations).astype(jnp.bfloat16)
```

```python
import jax
import jax.numpy as jnp
from jax import lax
from jax.experimental import pallas as pl
from jax.experimental.pallas import tpu as pltpu
from jax.sharding import PartitionSpec as P

reach = 2


def far_kernel(cols_ref, moments_ref, coupling_ref, rows_ref, out_ref, gathered, spread):
    slots = cols_ref.shape[0]
    rank = coupling_ref.shape[0]
    targets = out_ref.shape[0]

    def pick(slot, carry):
        source = pl.multiple_of(cols_ref[slot] * rank, rank)
        place = pl.multiple_of(slot * rank, rank)
        gathered[pl.ds(place, rank), :] = moments_ref[pl.ds(source, rank), :]
        return carry

    lax.fori_loop(0, slots, pick, 0)
    couplings = coupling_ref[...]
    rows = rows_ref[...]
    for target in range(targets):
        spread[target * rank : (target + 1) * rank, :] = jnp.where(
            rows == target, couplings, jnp.zeros_like(couplings)
        )
    incoming = jnp.dot(spread[...], gathered[...], preferred_element_type=jnp.float32)
    high = incoming.astype(jnp.bfloat16)
    rest = incoming - high.astype(jnp.float32)
    middle = rest.astype(jnp.bfloat16)
    low = (rest - middle.astype(jnp.float32)).astype(jnp.bfloat16)
    for target in range(targets):
        own = slice(target * rank, (target + 1) * rank)
        out_ref[target, 0:rank, :] = high[own]
        out_ref[target, rank : 2 * rank, :] = middle[own]
        out_ref[target, 2 * rank : 3 * rank, :] = low[own]


def far_incoming(far_cols, moments, coupling_rows, slot_rows, targets):
    rank, width = coupling_rows.shape
    excitations = moments.shape[1]
    return pl.pallas_call(
        far_kernel,
        grid_spec=pltpu.PrefetchScalarGridSpec(
            num_scalar_prefetch=1,
            grid=(1,),
            in_specs=[
                pl.BlockSpec(moments.shape, lambda i, *_: (0, 0)),
                pl.BlockSpec(coupling_rows.shape, lambda i, *_: (0, 0)),
                pl.BlockSpec(slot_rows.shape, lambda i, *_: (0, 0)),
            ],
            out_specs=pl.BlockSpec((targets, 3 * rank, excitations), lambda i, *_: (0, 0, 0)),
            scratch_shapes=[
                pltpu.VMEM((width, excitations), jnp.bfloat16),
                pltpu.VMEM((targets * rank, width), jnp.bfloat16),
            ],
        ),
        out_shape=jax.ShapeDtypeStruct((targets, 3 * rank, excitations), jnp.bfloat16),
        compiler_params=pltpu.CompilerParams(vmem_limit_bytes=32 * 2**20),
        cost_estimate=pl.CostEstimate(
            flops=2 * targets * rank * width * excitations,
            bytes_accessed=8 * 2**20,
            transcendentals=0,
        ),
        name="far_incoming",
    )(far_cols, moments, coupling_rows, slot_rows)


def near_kernel(
    place_ref, target_ref, blocks_ref, *rest
):
    parts = rest[: 2 * reach + 1]
    far_ref, basis_ref, out_ref = rest[2 * reach + 1 : 2 * reach + 4]
    held, sources, far, basis, result = rest[2 * reach + 4 : 2 * reach + 9]
    held_sem, source_sem, far_sem, basis_sem, result_sem = rest[2 * reach + 9 :]
    count = target_ref.shape[0]
    size = blocks_ref.shape[1]
    per_target = sources.shape[0] // size
    part_rows = parts[0].shape[0]

    def block_copy(step, source):
        slot = place_ref[target_ref[step] * per_target + source]
        return slot, pltpu.make_async_copy(
            blocks_ref.at[jnp.maximum(slot, 0)],
            held.at[step, :, pl.ds(source * size, size)],
            held_sem.at[step, source],
        )

    def far_copies(step):
        target = target_ref[step]
        return (
            pltpu.make_async_copy(far_ref.at[target], far.at[step], far_sem.at[step]),
            pltpu.make_async_copy(basis_ref.at[target], basis.at[step], basis_sem.at[step]),
        )

    def source_copy(index):
        return pltpu.make_async_copy(
            parts[index],
            sources.at[pl.ds(index * part_rows, part_rows), :],
            source_sem.at[index],
        )

    def result_copy(step):
        return pltpu.make_async_copy(result.at[step], out_ref.at[step], result_sem.at[step])

    for index in range(len(parts)):
        source_copy(index).start()

    def begin(step, carry):
        for copy in far_copies(step):
            copy.start()
        for source in range(per_target):
            slot, copy = block_copy(step, source)

            @pl.when(slot >= 0)
            def _():
                copy.start()

            @pl.when(slot < 0)
            def _():
                held[step, :, source * size : (source + 1) * size] = jnp.zeros(
                    (size, size), held.dtype
                )

        return carry

    lax.fori_loop(0, count, begin, 0)
    for index in range(len(parts)):
        source_copy(index).wait()

    def work(step, carry):
        for copy in far_copies(step):
            copy.wait()
        for source in range(per_target):
            slot, copy = block_copy(step, source)

            @pl.when(slot >= 0)
            def _():
                copy.wait()

        total = jnp.dot(held[step], sources[...], preferred_element_type=jnp.float32)
        total = total + jnp.dot(basis[step], far[step], preferred_element_type=jnp.float32)
        result[step] = total.astype(result.dtype)
        result_copy(step).start()
        return carry

    lax.fori_loop(0, count, work, 0)

    def finish(step, carry):
        result_copy(step).wait()
        return carry

    lax.fori_loop(0, count, finish, 0)


def near_terms(place, targets, blocks, parts, far, basis):
    count = targets.shape[0]
    size = blocks.shape[1]
    part_rows, excitations = parts[0].shape
    depth = part_rows * len(parts)
    anywhere = pl.BlockSpec(memory_space=pl.ANY)
    return pl.pallas_call(
        near_kernel,
        grid_spec=pltpu.PrefetchScalarGridSpec(
            num_scalar_prefetch=2,
            grid=(1,),
            in_specs=[anywhere] * (3 + len(parts)),
            out_specs=anywhere,
            scratch_shapes=[
                pltpu.VMEM((count, size, depth), jnp.bfloat16),
                pltpu.VMEM((depth, excitations), jnp.bfloat16),
                pltpu.VMEM((count,) + far.shape[1:], jnp.bfloat16),
                pltpu.VMEM((count,) + basis.shape[1:], jnp.bfloat16),
                pltpu.VMEM((count, size, excitations), jnp.bfloat16),
                pltpu.SemaphoreType.DMA((count, depth // size)),
                pltpu.SemaphoreType.DMA((len(parts),)),
                pltpu.SemaphoreType.DMA((count,)),
                pltpu.SemaphoreType.DMA((count,)),
                pltpu.SemaphoreType.DMA((count,)),
            ],
        ),
        out_shape=jax.ShapeDtypeStruct((count, size, excitations), jnp.bfloat16),
        compiler_params=pltpu.CompilerParams(vmem_limit_bytes=40 * 2**20),
        cost_estimate=pl.CostEstimate(
            flops=2 * count * size * depth * excitations,
            bytes_accessed=2 * (count * size * depth + depth * excitations),
            transcendentals=0,
        ),
        name="near_terms",
    )(place, targets, blocks, *parts, far, basis)


def add(*terms):
    total = terms[0].astype(jnp.float32)
    for term in terms[1:]:
        total = total + term.astype(jnp.float32)
    return total.astype(jnp.bfloat16)


def shards(
    charges,
    send_order,
    near_rows,
    near_cols,
    near_count,
    near_blocks,
    far_rows,
    far_cols,
    far_count,
    couplings,
    row_basis,
    col_basis,
):
    row_count = lax.axis_size("row")
    col_count = lax.axis_size("col")
    device_count = row_count * col_count
    panels, excitations = charges.shape
    segment = panels // device_count
    owned, rank, leaf = col_basis.shape
    targets = row_basis.shape[0]
    window = (2 * reach + 1) * owned
    row = lax.axis_index("row")
    col = lax.axis_index("col")

    slots = jnp.arange(near_rows.shape[1], dtype=jnp.int32)
    pair = near_rows[0] * window + near_cols[0] - (row - reach) * owned
    pair = jnp.where(slots < near_count[0], pair, -1)
    wanted = jnp.arange(targets * window, dtype=jnp.int32)
    place = jnp.max(jnp.where(pair[None, :] == wanted[:, None], slots[None, :], -1), axis=1)

    far_slots = far_rows.shape[1]
    far_target = jnp.where(
        jnp.arange(far_slots, dtype=jnp.int32) < far_count[0], far_rows[0], -1
    )
    slot_rows = jnp.repeat(far_target, rank)[None, :]
    coupling_rows = couplings[0].transpose(1, 0, 2).reshape(rank, far_slots * rank)
    basis = jnp.tile(row_basis.transpose(0, 2, 1), (1, 1, 3))

    outgoing = jnp.take(charges, send_order[0], axis=0)
    incoming = lax.all_to_all(
        outgoing.reshape(device_count, segment, excitations),
        ("row", "col"),
        split_axis=0,
        concat_axis=0,
        tiled=True,
    )
    slab = incoming.reshape(panels, excitations)
    moments = (
        jnp.einsum(
            "gkb,gbr->gkr",
            col_basis,
            slab.reshape(owned, leaf, excitations),
            preferred_element_type=jnp.float32,
        )
        .astype(jnp.bfloat16)
        .reshape(owned * rank, excitations)
    )

    def row_shift(value, step):
        return lax.ppermute(value, "row", [(i, (i + step) % row_count) for i in range(row_count)])

    all_moments = lax.all_gather(moments, "row", axis=0, tiled=True)
    below, above = [slab], [slab]
    for _ in range(reach):
        below.append(row_shift(below[-1], 1))
        above.append(row_shift(above[-1], -1))
    parts = below[:0:-1] + above
    far = far_incoming(far_cols[0], all_moments, coupling_rows, slot_rows, targets)

    chips = col_count // 2
    chip, core = col // 2, col % 2
    each = jnp.arange(owned, dtype=jnp.int32)

    def clusters(chip_step, which):
        return (((chip + chip_step) % chips) * 2 + which) * owned + each

    def order(*chip_steps):
        return jnp.concatenate(
            [clusters(step, 1 - core) for step in chip_steps]
            + [clusters(step, core) for step in chip_steps]
        )

    def other_core(value):
        return lax.ppermute(value, "col", [(i, i ^ 1) for i in range(col_count)])

    def chip_shift(value, step):
        return lax.ppermute(
            value, "col", [(i, (i + 2 * step) % col_count) for i in range(col_count)]
        )

    def both_cores(terms):
        half = terms.shape[0] // 2
        return terms[half:], other_core(terms[:half])

    opposite = add(*both_cores(near_terms(place, order(2), near_blocks[0], parts, far, basis)))
    opposite, place = lax.optimization_barrier((opposite, place))
    from_below = chip_shift(opposite[:1], 1)
    from_above = chip_shift(opposite[1:], -1)
    kept, got = both_cores(near_terms(place, order(1, -1), near_blocks[0], parts, far, basis))
    zero = jnp.zeros_like(from_below)
    passing = jnp.concatenate([from_below, zero, zero, from_above])
    sides = add(kept, got, passing)
    sides, place = lax.optimization_barrier((sides, place))
    side_below = chip_shift(sides[:owned], 1)
    side_above = chip_shift(sides[owned:], -1)
    kept, got = both_cores(near_terms(place, order(0), near_blocks[0], parts, far, basis))
    return add(kept, got, side_below, side_above).reshape(panels, excitations)


def solution(mesh):
    placed = (
        P(("row", "col"), None),
        P(("row", "col"), None),
        P(("row", "col"), None),
        P(("row", "col"), None),
        P(("row", "col")),
        P(("row", "col"), None, None, None),
        P(("row", "col"), None),
        P(("row", "col"), None),
        P(("row", "col")),
        P(("row", "col"), None, None, None),
        P("row", None, None),
        P(("row", "col"), None, None),
    )
    return jax.shard_map(
        shards, mesh=mesh, in_specs=placed, out_specs=P(("row", "col"), None), check_vma=False
    )
```

```python
import jax
import jax.numpy as jnp
from jax import lax
from jax.experimental import pallas as pl
from jax.experimental.pallas import tpu as pltpu
from jax.sharding import PartitionSpec as P

reach = 2
across = 4


def in_hbm(*values):
    return [pltpu.with_memory_space_constraint(value, pltpu.HBM) for value in values]


def far_kernel(cols_ref, *rest):
    parts = rest[:-9]
    coupling_ref, rows_ref, out_ref, moments, gathered, spread, part_sem, result, out_sem = rest[-9:]
    slots = cols_ref.shape[0]
    rank = coupling_ref.shape[0]
    targets = out_ref.shape[0] // rank
    sizes = [part.shape[0] for part in parts]

    def part_copy(index):
        here = pl.ds(sum(sizes[:index]), sizes[index])
        return pltpu.make_async_copy(parts[index], moments.at[here, :], part_sem.at[index])

    for index in range(len(parts)):
        part_copy(index).start()
    couplings = coupling_ref[...]
    rows = rows_ref[...]
    for target in range(targets):
        spread[target * rank : (target + 1) * rank, :] = jnp.where(
            rows == target, couplings, jnp.zeros_like(couplings)
        )
    for index in range(len(parts)):
        part_copy(index).wait()

    def pick(slot, carry):
        source = pl.multiple_of(cols_ref[slot] * rank, rank)
        place = pl.multiple_of(slot * rank, rank)
        gathered[pl.ds(place, rank), :] = moments[pl.ds(source, rank), :]
        return carry

    lax.fori_loop(0, slots, pick, 0, unroll=4)
    incoming = jnp.dot(spread[...], gathered[...], preferred_element_type=jnp.float32)
    result[...] = incoming.astype(jnp.bfloat16)
    copy = pltpu.make_async_copy(result, out_ref, out_sem)
    copy.start()
    copy.wait()


def far_incoming(far_cols, moment_parts, coupling_rows, slot_rows, targets):
    rank, width = coupling_rows.shape
    depth = sum(part.shape[0] for part in moment_parts)
    excitations = moment_parts[0].shape[1]
    shape = (targets * rank, excitations)
    anywhere = pl.BlockSpec(memory_space=pltpu.HBM)
    return pl.pallas_call(
        far_kernel,
        grid_spec=pltpu.PrefetchScalarGridSpec(
            num_scalar_prefetch=1,
            grid=(1,),
            in_specs=[anywhere] * len(moment_parts)
            + [
                pl.BlockSpec(coupling_rows.shape, lambda i, *_: (0, 0)),
                pl.BlockSpec(slot_rows.shape, lambda i, *_: (0, 0)),
            ],
            out_specs=anywhere,
            scratch_shapes=[
                pltpu.VMEM((depth, excitations), jnp.bfloat16),
                pltpu.VMEM((width, excitations), jnp.bfloat16),
                pltpu.VMEM((targets * rank, width), jnp.bfloat16),
                pltpu.SemaphoreType.DMA((len(moment_parts),)),
                pltpu.VMEM(shape, jnp.bfloat16),
                pltpu.SemaphoreType.DMA,
            ],
        ),
        out_shape=pltpu.HBM(shape, jnp.bfloat16),
        compiler_params=pltpu.CompilerParams(vmem_limit_bytes=12 * 2**20),
        cost_estimate=pl.CostEstimate(
            flops=2 * targets * rank * width * excitations,
            bytes_accessed=8 * 2**20,
            transcendentals=0,
        ),
        name="far_incoming",
    )(far_cols, *moment_parts, coupling_rows, slot_rows)


def near_terms(place, targets, blocks, parts, columns, splits, window, partial=None):
    count = targets.shape[0]
    size = blocks.shape[1]
    part_rows, excitations = parts[0].shape
    per_target = len(columns)
    depth = per_target * size
    ahead = min(4, count)
    finishing = partial is not None
    starts = [sum(splits[:index]) for index in range(len(splits))]

    def kernel(place_ref, target_ref, blocks_ref, *rest):
        rest = list(rest)
        part_refs = [rest.pop(0) for _ in parts]
        if finishing:
            partial_ref = rest.pop(0)
        out_refs = [rest.pop(0) for _ in splits]
        held, sources, result, held_sem, source_sem, result_sem = [rest.pop(0) for _ in range(6)]
        if finishing:
            running, running_sem = rest

        def source_copy(index):
            return pltpu.make_async_copy(
                part_refs[index],
                sources.at[pl.ds(index * part_rows, part_rows), :],
                source_sem.at[index],
            )

        def running_copy(step):
            return pltpu.make_async_copy(
                partial_ref.at[target_ref[step]], running.at[step], running_sem.at[step]
            )

        def begin(step):
            first = target_ref[step] * window
            for index, column in enumerate(columns):
                slot = jnp.maximum(place_ref[first + column], 0)
                pltpu.make_async_copy(
                    blocks_ref.at[slot], held.at[step * per_target + index], held_sem.at[step]
                ).start()
            if finishing:
                running_copy(step).start()

        def work(step):
            first = target_ref[step] * window
            pltpu.make_async_copy(
                blocks_ref.at[pl.ds(0, per_target)],
                held.at[pl.ds(step * per_target, per_target)],
                held_sem.at[step],
            ).wait()
            if finishing:
                running_copy(step).wait()
            total = None
            for index, column in enumerate(columns):
                here = jnp.where(
                    place_ref[first + column] >= 0, step * per_target + index, count * per_target
                )
                product = jnp.dot(
                    held[here],
                    sources[index * size : (index + 1) * size, :],
                    preferred_element_type=jnp.float32,
                )
                total = product if total is None else total + product
            if finishing:
                total = total + running[step].astype(jnp.float32)
            result[step] = total.astype(result.dtype)

        begin(0)
        for index in range(len(parts)):
            source_copy(index).start()
        for step in range(1, ahead):
            begin(step)
        held[count * per_target] = jnp.zeros((size, size), held.dtype)
        for index in range(len(parts)):
            source_copy(index).wait()

        def result_copy(index, step):
            return pltpu.make_async_copy(
                result.at[step], out_refs[index].at[step - starts[index]], result_sem.at[step]
            )

        for index in range(len(splits)):
            first, last = starts[index], starts[index] + splits[index]

            def both(step, carry):
                begin(step + ahead)
                return only(step, carry)

            def only(step, carry):
                work(step)
                result_copy(index, step).start()
                return carry

            middle = min(max(first, count - ahead), last)
            lax.fori_loop(first, middle, both, 0)
            lax.fori_loop(middle, last, only, 0)
        for index in range(len(splits)):

            def end(step, carry):
                result_copy(index, step).wait()
                return carry

            lax.fori_loop(starts[index], starts[index] + splits[index], end, 0)

    anywhere = pl.BlockSpec(memory_space=pltpu.HBM)
    extras = (partial,) if finishing else ()
    scratch = [
        pltpu.VMEM((count * per_target + 1, size, size), jnp.bfloat16),
        pltpu.VMEM((depth, excitations), jnp.bfloat16),
        pltpu.VMEM((count, size, excitations), jnp.bfloat16),
        pltpu.SemaphoreType.DMA((count,)),
        pltpu.SemaphoreType.DMA((len(parts),)),
        pltpu.SemaphoreType.DMA((count,)),
    ]
    if finishing:
        scratch += [
            pltpu.VMEM((count, size, excitations), jnp.bfloat16),
            pltpu.SemaphoreType.DMA((count,)),
        ]
    return pl.pallas_call(
        kernel,
        grid_spec=pltpu.PrefetchScalarGridSpec(
            num_scalar_prefetch=2,
            grid=(1,),
            in_specs=[anywhere] * (1 + len(parts) + len(extras)),
            out_specs=[anywhere] * len(splits),
            scratch_shapes=scratch,
        ),
        out_shape=[
            pltpu.HBM((split, size, excitations), jnp.bfloat16) for split in splits
        ],
        compiler_params=pltpu.CompilerParams(
            vmem_limit_bytes=2 * size * (count * per_target * size + (depth + 2 * count * size) * 2)
            + 4 * 2**20
        ),
        cost_estimate=pl.CostEstimate(
            flops=2 * count * size * depth * excitations,
            bytes_accessed=2 * (count * size * depth + depth * excitations),
            transcendentals=0,
        ),
        name="near_rest" if finishing else "near_first",
    )(place, targets, *in_hbm(blocks), *parts, *in_hbm(*extras))


def finish_kernel(*rest):
    kept_ref, got_ref, below_late, above_late, below_early, above_early, *far_refs = rest[:-2]
    basis_ref, out_ref = rest[-2:]
    owned = out_ref.shape[0]
    rank = far_refs[0].shape[0] // owned
    sides = [[below_late, above_early], [below_early, above_late]]
    for cluster in range(owned):
        rows = slice(cluster * rank, (cluster + 1) * rank)
        incoming = far_refs[0][rows, :].astype(jnp.float32)
        for far_ref in far_refs[1:]:
            incoming = incoming + far_ref[rows, :].astype(jnp.float32)
        high = incoming.astype(jnp.bfloat16)
        left = incoming - high.astype(jnp.float32)
        middle = left.astype(jnp.bfloat16)
        low = (left - middle.astype(jnp.float32)).astype(jnp.bfloat16)
        total = jnp.dot(
            basis_ref[cluster],
            jnp.concatenate([high, middle, low]),
            preferred_element_type=jnp.float32,
        )
        for part in (kept_ref[cluster], got_ref[cluster], sides[cluster][0][0], sides[cluster][1][0]):
            total = total + part.astype(jnp.float32)
        out_ref[cluster] = total.astype(out_ref.dtype)


def finish(kept, got, late, early, far_parts, basis):
    operands = [kept, got, *late, *early, *far_parts, basis]
    whole = pl.BlockSpec(memory_space=pltpu.VMEM)
    return pl.pallas_call(
        finish_kernel,
        in_specs=[whole] * len(operands),
        out_specs=whole,
        out_shape=jax.ShapeDtypeStruct(kept.shape, jnp.bfloat16),
        compiler_params=pltpu.CompilerParams(vmem_limit_bytes=16 * 2**20),
        cost_estimate=pl.CostEstimate(
            flops=2 * kept.size * basis.shape[2],
            bytes_accessed=2 * 5 * kept.size,
            transcendentals=0,
        ),
        name="finish",
    )(*operands)


def add(*terms):
    total = terms[0].astype(jnp.float32)
    for term in terms[1:]:
        total = total + term.astype(jnp.float32)
    return total.astype(jnp.bfloat16)


def shards(
    charges,
    send_order,
    near_rows,
    near_cols,
    near_count,
    near_blocks,
    far_rows,
    far_cols,
    far_count,
    couplings,
    row_basis,
    col_basis,
):
    row_count = lax.axis_size("row")
    col_count = lax.axis_size("col")
    device_count = row_count * col_count
    panels, excitations = charges.shape
    segment = panels // device_count
    owned, rank, leaf = col_basis.shape
    targets = row_basis.shape[0]
    window = (2 * reach + 1) * owned
    row = lax.axis_index("row")
    col = lax.axis_index("col")

    outgoing = charges.at[send_order[0]].get(mode="promise_in_bounds")
    incoming = lax.all_to_all(
        outgoing.reshape(device_count, segment, excitations),
        ("row", "col"),
        split_axis=0,
        concat_axis=0,
        tiled=True,
    )
    slab = incoming.reshape(panels, excitations)
    (
        slab,
        near_rows,
        near_cols,
        near_count,
        far_rows,
        far_cols,
        far_count,
        couplings,
        row_basis,
    ) = lax.optimization_barrier(
        (
            slab,
            near_rows,
            near_cols,
            near_count,
            far_rows,
            far_cols,
            far_count,
            couplings,
            row_basis,
        )
    )
    def row_shift(value, step):
        return lax.ppermute(value, "row", [(i, (i + step) % row_count) for i in range(row_count)])

    def line_shift(value, step):
        return lax.ppermute(
            value,
            "row",
            [(i, i // across * across + (i + step) % across) for i in range(row_count)],
        )

    def other_core(value):
        return lax.ppermute(value, "col", [(i, i ^ 1) for i in range(col_count)])

    def chip_shift(value, step):
        return lax.ppermute(
            value, "col", [(i, (i + 2 * step) % col_count) for i in range(col_count)]
        )

    below = row_shift(slab, 1)
    above = row_shift(slab, -1)
    slots = jnp.arange(near_rows.shape[1], dtype=jnp.int32)
    pair = near_rows[0] * window + near_cols[0] - (row - reach) * owned
    pair = jnp.where(slots < near_count[0], pair, -1)
    wanted = jnp.arange(targets * window, dtype=jnp.int32)
    place = jnp.max(jnp.where(pair[None, :] == wanted[:, None], slots[None, :], -1), axis=1)

    far_slots = far_rows.shape[1]
    far_target = jnp.where(
        jnp.arange(far_slots, dtype=jnp.int32) < far_count[0], far_rows[0], -1
    )
    coupling_rows = couplings[0].transpose(1, 0, 2).reshape(rank, far_slots * rank)
    own_basis = lax.dynamic_slice_in_dim(row_basis, col * owned, owned, 0)
    own_basis = jnp.tile(own_basis.transpose(0, 2, 1), (1, 1, 3))
    far_row = far_cols[0] // owned
    far_line = (far_row // across - row // across) % (row_count // across)
    far_place = (far_row - row) % across
    far_source = (far_line * across + far_place) * owned + far_cols[0] % owned

    chips = col_count // 2
    chip, core = col // 2, col % 2
    each = jnp.arange(owned, dtype=jnp.int32)

    def clusters(chip_step, which):
        return (((chip + chip_step) % chips) * 2 + which) * owned + each

    def order(*chip_steps):
        return jnp.concatenate(
            [clusters(step, 1 - core) for step in chip_steps]
            + [clusters(step, core) for step in chip_steps]
        )

    far_chip = (far_target // (2 * owned) - chip) % chips
    far_core = (far_target // owned + 1 - core) % 2
    far_place = (far_core * chips + far_chip) * owned + far_target % owned
    far_place = jnp.where(far_target >= 0, far_place, -1)
    slot_rows = jnp.repeat(far_place, rank)[None, :]

    blocks = near_blocks[0]
    everyone = jnp.arange(targets, dtype=jnp.int32)
    middle = list(range(reach * owned, (reach + 1) * owned))
    inner = [column for column in range(owned, window - owned) if column not in middle]
    outer = list(range(owned)) + list(range(window - owned, window))
    (partial,) = near_terms(place, everyone, blocks, [slab], middle, [targets], window)
    slab, below, above, partial = lax.optimization_barrier((slab, below, above, partial))
    moments = (
        jnp.einsum(
            "gkb,gbr->gkr",
            col_basis,
            slab.reshape(owned, leaf, excitations),
            preferred_element_type=jnp.float32,
        )
        .astype(jnp.bfloat16)
        .reshape(owned * rank, excitations)
    )
    of_line = jnp.concatenate([moments] + [line_shift(moments, -step) for step in range(1, across)])

    below_more = row_shift(below, 1)
    above_more = row_shift(above, -1)
    (partial,) = near_terms(
        place, everyone, blocks, [below, above], inner, [targets], window, partial
    )

    def rest(*chip_steps):
        return near_terms(
            place,
            order(*chip_steps),
            blocks,
            [below_more, above_more],
            outer,
            [owned * len(chip_steps)] + [owned] * len(chip_steps),
            window,
            partial,
        )

    of_line, partial = lax.optimization_barrier((of_line, partial))
    next_line = row_shift(of_line, -across)
    last_line = row_shift(of_line, across)
    sent, kept = rest(2)
    sent, next_line, last_line = lax.optimization_barrier((sent, next_line, last_line))
    half = of_line.shape[0] // 2
    second_line = [row_shift(next_line[:half], -across), row_shift(last_line[half:], across)]
    opposite = add(kept, other_core(sent))
    opposite, place = lax.optimization_barrier((opposite, place))
    from_below = chip_shift(opposite[:1], 1)
    from_above = chip_shift(opposite[1:], -1)
    sent, kept_up, kept_down = rest(1, -1)
    sent, from_below, from_above, second_line = lax.optimization_barrier(
        (sent, from_below, from_above, second_line)
    )
    got = other_core(sent)
    kept_up, second_line = lax.optimization_barrier((kept_up, second_line))
    incoming = far_incoming(
        far_source,
        [of_line, next_line, *second_line, last_line],
        coupling_rows,
        slot_rows,
        targets,
    )
    incoming, got = lax.optimization_barrier((incoming, got))
    early = [add(kept_up[1:], got[1:2]), add(kept_down[:1], got[owned : owned + 1])]
    late = [add(kept_up[:1], got[:1], from_below), add(kept_down[1:], got[owned + 1 :], from_above)]
    early, late, place, incoming = lax.optimization_barrier((early, late, place, incoming))
    side_early = [chip_shift(early[0], 1), chip_shift(early[1], -1)]
    far_half = incoming.shape[0] // 2
    far_got = other_core(incoming[:far_half])
    sent, kept = rest(0)
    sent, far_got, side_early, late = lax.optimization_barrier((sent, far_got, side_early, late))
    side_late = [chip_shift(late[0], 1), chip_shift(late[1], -1)]
    far = add(incoming[far_half:], far_got).reshape(chips, owned * rank, excitations)
    far_parts = [far[0]] + [chip_shift(far[step], step) for step in range(1, chips)]
    got = other_core(sent)
    return finish(kept, got, side_late, side_early, far_parts, own_basis).reshape(
        panels, excitations
    )


def solution(mesh):
    placed = (
        P(("row", "col"), None),
        P(("row", "col"), None),
        P(("row", "col"), None),
        P(("row", "col"), None),
        P(("row", "col")),
        P(("row", "col"), None, None, None),
        P(("row", "col"), None),
        P(("row", "col"), None),
        P(("row", "col")),
        P(("row", "col"), None, None, None),
        P("row", None, None),
        P(("row", "col"), None, None),
    )
    return jax.shard_map(
        shards, mesh=mesh, in_specs=placed, out_specs=P(("row", "col"), None), check_vma=False
    )
```

```python
import jax
import jax.numpy as jnp
from jax import lax
from jax.experimental import pallas as pl
from jax.experimental.pallas import tpu as pltpu
from jax.sharding import PartitionSpec as P

reach = 2


def in_hbm(*values):
    return [pltpu.with_memory_space_constraint(value, pltpu.HBM) for value in values]


def far_incoming(cols_ref, moments, coupling_ref, rows_ref, gathered, spread, arrived):
    slots = cols_ref.shape[0]
    rank = coupling_ref.shape[0]
    couplings = coupling_ref[...]
    rows = rows_ref[...]
    for target in range(spread.shape[0] // rank):
        spread[target * rank : (target + 1) * rank, :] = jnp.where(
            rows == target, couplings, jnp.zeros_like(couplings)
        )
    arrived()

    def pick(slot, carry):
        source = pl.multiple_of(cols_ref[slot] * rank, rank)
        here = pl.multiple_of(slot * rank, rank)
        gathered[pl.ds(here, rank), :] = moments[pl.ds(source, rank), :]
        return carry

    lax.fori_loop(0, slots, pick, 0, unroll=4)
    return jnp.dot(spread[...], gathered[...], preferred_element_type=jnp.float32)


def near_terms(place, targets, blocks, parts, columns, splits, window, partial=None, far=None):
    count = targets.shape[0]
    size = blocks.shape[1]
    part_rows, excitations = parts[0].shape
    per_target = len(columns)
    depth = per_target * size
    ahead = min(4, count)
    finishing = partial is not None
    far_cols, moment_parts, *coupling = far or (None, [])
    moment_sizes = [part.shape[0] for part in moment_parts]
    starts = [sum(splits[:index]) for index in range(len(splits))]

    def kernel(place_ref, target_ref, *rest):
        rest = list(rest)
        if far:
            cols_ref = rest.pop(0)
        blocks_ref = rest.pop(0)
        part_refs = [rest.pop(0) for _ in parts]
        if finishing:
            partial_ref = rest.pop(0)
        if far:
            moment_refs = [rest.pop(0) for _ in moment_parts]
            coupling_ref, rows_ref = rest.pop(0), rest.pop(0)
        out_refs = [rest.pop(0) for _ in splits]
        if far:
            far_ref = rest.pop(0)
        held, sources, result, held_sem, source_sem, result_sem = [rest.pop(0) for _ in range(6)]
        if finishing:
            running, running_sem = rest.pop(0), rest.pop(0)
        if far:
            moments, gathered, spread, moment_sem = rest

        def source_copy(index):
            return pltpu.make_async_copy(
                part_refs[index],
                sources.at[pl.ds(index * part_rows, part_rows), :],
                source_sem.at[index],
            )

        def running_copy(step):
            return pltpu.make_async_copy(
                partial_ref.at[target_ref[step]], running.at[step], running_sem.at[step]
            )

        def moment_copy(index):
            here = pl.ds(sum(moment_sizes[:index]), moment_sizes[index])
            return pltpu.make_async_copy(
                moment_refs[index], moments.at[here, :], moment_sem.at[index]
            )

        def far_copies():
            return (
                pltpu.make_async_copy(
                    result.at[count], out_refs[0].at[splits[0]], result_sem.at[count]
                ),
                pltpu.make_async_copy(
                    result.at[count + 1], far_ref.at[0], result_sem.at[count + 1]
                ),
            )

        def moments_arrived():
            for index in range(len(moment_parts)):
                moment_copy(index).wait()

        def begin(step):
            first = target_ref[step] * window
            for index, column in enumerate(columns):
                slot = jnp.maximum(place_ref[first + column], 0)
                pltpu.make_async_copy(
                    blocks_ref.at[slot], held.at[step * per_target + index], held_sem.at[step]
                ).start()
            if finishing:
                running_copy(step).start()

        def work(step):
            first = target_ref[step] * window
            pltpu.make_async_copy(
                blocks_ref.at[pl.ds(0, per_target)],
                held.at[pl.ds(step * per_target, per_target)],
                held_sem.at[step],
            ).wait()
            if finishing:
                running_copy(step).wait()
            total = None
            for index, column in enumerate(columns):
                here = jnp.where(
                    place_ref[first + column] >= 0, step * per_target + index, count * per_target
                )
                product = jnp.dot(
                    held[here],
                    sources[index * size : (index + 1) * size, :],
                    preferred_element_type=jnp.float32,
                )
                total = product if total is None else total + product
            if finishing:
                total = total + running[step].astype(jnp.float32)
            result[step] = total.astype(result.dtype)

        begin(0)
        for index in range(len(parts)):
            source_copy(index).start()
        for index in range(len(moment_parts)):
            moment_copy(index).start()
        for step in range(1, ahead):
            begin(step)
        held[count * per_target] = jnp.zeros((size, size), held.dtype)
        if far:
            incoming = far_incoming(
                cols_ref, moments, coupling_ref, rows_ref, gathered, spread, moments_arrived
            )
            result[count] = incoming[:size].astype(result.dtype)
            result[count + 1] = incoming[size:].astype(result.dtype)
            for copy in far_copies():
                copy.start()
        for index in range(len(parts)):
            source_copy(index).wait()

        def result_copy(index, step):
            return pltpu.make_async_copy(
                result.at[step], out_refs[index].at[step - starts[index]], result_sem.at[step]
            )

        for index in range(len(splits)):
            first, last = starts[index], starts[index] + splits[index]

            def both(step, carry):
                begin(step + ahead)
                return only(step, carry)

            def only(step, carry):
                work(step)
                result_copy(index, step).start()
                return carry

            middle = min(max(first, count - ahead), last)
            lax.fori_loop(first, middle, both, 0)
            lax.fori_loop(middle, last, only, 0)
        for index in range(len(splits)):

            def end(step, carry):
                result_copy(index, step).wait()
                return carry

            lax.fori_loop(starts[index], starts[index] + splits[index], end, 0)
        if far:
            for copy in far_copies():
                copy.wait()

    anywhere = pl.BlockSpec(memory_space=pltpu.HBM)
    extras = (partial,) if finishing else ()
    more = 2 if far else 0
    scratch = [
        pltpu.VMEM((count * per_target + 1, size, size), jnp.bfloat16),
        pltpu.VMEM((depth, excitations), jnp.bfloat16),
        pltpu.VMEM((count + more, size, excitations), jnp.bfloat16),
        pltpu.SemaphoreType.DMA((count,)),
        pltpu.SemaphoreType.DMA((len(parts),)),
        pltpu.SemaphoreType.DMA((count + more,)),
    ]
    if finishing:
        scratch += [
            pltpu.VMEM((count, size, excitations), jnp.bfloat16),
            pltpu.SemaphoreType.DMA((count,)),
        ]
    shapes = [(split, size, excitations) for split in splits]
    coupling_specs = [pl.BlockSpec(item.shape, lambda i, *_: (0, 0)) for item in coupling]
    if far:
        shapes[0] = (splits[0] + 1, size, excitations)
        shapes.append((1, size, excitations))
        scratch += [
            pltpu.VMEM((sum(moment_sizes), excitations), jnp.bfloat16),
            pltpu.VMEM((coupling[0].shape[1], excitations), jnp.bfloat16),
            pltpu.VMEM((2 * size, coupling[0].shape[1]), jnp.bfloat16),
            pltpu.SemaphoreType.DMA((len(moment_parts),)),
        ]
    return pl.pallas_call(
        kernel,
        grid_spec=pltpu.PrefetchScalarGridSpec(
            num_scalar_prefetch=3 if far else 2,
            grid=(1,),
            in_specs=[anywhere] * (1 + len(parts) + len(extras) + len(moment_parts))
            + coupling_specs,
            out_specs=[anywhere] * len(shapes),
            scratch_shapes=scratch,
        ),
        out_shape=[pltpu.HBM(shape, jnp.bfloat16) for shape in shapes],
        compiler_params=pltpu.CompilerParams(
            vmem_limit_bytes=2 * size * (count * per_target * size + (depth + 2 * count * size) * 2)
            + (14 if far else 4) * 2**20
        ),
        cost_estimate=pl.CostEstimate(
            flops=2 * count * size * depth * excitations,
            bytes_accessed=2 * (count * size * depth + depth * excitations),
            transcendentals=0,
        ),
        name="near_rest" if finishing else "near_first",
    )(
        place,
        targets,
        *([far_cols] if far else []),
        *in_hbm(blocks),
        *parts,
        *in_hbm(*extras),
        *moment_parts,
        *coupling,
    )


def finish_kernel(
    kept_ref, got_ref, below_late, above_late, below_early, above_early, far_ref, basis_ref, out_ref
):
    owned, size, _ = out_ref.shape
    rank = basis_ref.shape[2] // 3
    sides = [[below_late, above_early], [below_early, above_late]]
    relayed = [below_late, above_late]
    for cluster in range(owned):
        rows = slice(size + cluster * rank, size + (cluster + 1) * rank)
        incoming = far_ref[cluster * rank : (cluster + 1) * rank, :].astype(jnp.float32)
        incoming = incoming + below_early[rows, :].astype(jnp.float32)
        incoming = incoming + above_early[rows, :].astype(jnp.float32)
        incoming = incoming + relayed[cluster][size : size + rank, :].astype(jnp.float32)
        high = incoming.astype(jnp.bfloat16)
        left = incoming - high.astype(jnp.float32)
        middle = left.astype(jnp.bfloat16)
        low = (left - middle.astype(jnp.float32)).astype(jnp.bfloat16)
        total = jnp.dot(
            basis_ref[cluster],
            jnp.concatenate([high, middle, low]),
            preferred_element_type=jnp.float32,
        )
        total = total + kept_ref[cluster].astype(jnp.float32)
        total = total + got_ref[cluster].astype(jnp.float32)
        for side in sides[cluster]:
            total = total + side[0:size, :].astype(jnp.float32)
        out_ref[cluster] = total.astype(out_ref.dtype)


def finish(kept, got, late, early, far, basis):
    operands = [kept, got, *late, *early, far, basis]
    whole = pl.BlockSpec(memory_space=pltpu.VMEM)
    return pl.pallas_call(
        finish_kernel,
        in_specs=[whole] * len(operands),
        out_specs=whole,
        out_shape=jax.ShapeDtypeStruct(kept.shape, jnp.bfloat16),
        compiler_params=pltpu.CompilerParams(vmem_limit_bytes=16 * 2**20),
        cost_estimate=pl.CostEstimate(
            flops=2 * kept.size * basis.shape[2],
            bytes_accessed=2 * 5 * kept.size,
            transcendentals=0,
        ),
        name="finish",
    )(*operands)


def add(*terms):
    total = terms[0].astype(jnp.float32)
    for term in terms[1:]:
        total = total + term.astype(jnp.float32)
    return total.astype(jnp.bfloat16)


def shards(
    charges,
    send_order,
    near_rows,
    near_cols,
    near_count,
    near_blocks,
    far_rows,
    far_cols,
    far_count,
    couplings,
    row_basis,
    col_basis,
):
    row_count = lax.axis_size("row")
    col_count = lax.axis_size("col")
    device_count = row_count * col_count
    panels, excitations = charges.shape
    segment = panels // device_count
    owned, rank, leaf = col_basis.shape
    targets = row_basis.shape[0]
    window = (2 * reach + 1) * owned
    row = lax.axis_index("row")
    col = lax.axis_index("col")

    outgoing = charges.at[send_order[0]].get(mode="promise_in_bounds")
    incoming = lax.all_to_all(
        outgoing.reshape(device_count, segment, excitations),
        ("row", "col"),
        split_axis=0,
        concat_axis=0,
        tiled=True,
    )
    slab = incoming.reshape(panels, excitations)
    (
        slab,
        near_rows,
        near_cols,
        near_count,
        far_rows,
        far_cols,
        far_count,
        couplings,
        row_basis,
    ) = lax.optimization_barrier(
        (
            slab,
            near_rows,
            near_cols,
            near_count,
            far_rows,
            far_cols,
            far_count,
            couplings,
            row_basis,
        )
    )
    def row_shift(value, step):
        return lax.ppermute(value, "row", [(i, (i + step) % row_count) for i in range(row_count)])

    def other_core(value):
        return lax.ppermute(value, "col", [(i, i ^ 1) for i in range(col_count)])

    def chip_shift(value, step):
        return lax.ppermute(
            value, "col", [(i, (i + 2 * step) % col_count) for i in range(col_count)]
        )

    below = row_shift(slab, 1)
    above = row_shift(slab, -1)
    moments = (
        jnp.einsum(
            "gkb,gbr->gkr",
            col_basis,
            slab.reshape(owned, leaf, excitations),
            preferred_element_type=jnp.float32,
        )
        .astype(jnp.bfloat16)
        .reshape(owned * rank, excitations)
    )
    slots = jnp.arange(near_rows.shape[1], dtype=jnp.int32)
    pair = near_rows[0] * window + near_cols[0] - (row - reach) * owned
    pair = jnp.where(slots < near_count[0], pair, -1)
    wanted = jnp.arange(targets * window, dtype=jnp.int32)
    place = jnp.max(jnp.where(pair[None, :] == wanted[:, None], slots[None, :], -1), axis=1)

    far_slots = far_rows.shape[1]
    far_target = jnp.where(
        jnp.arange(far_slots, dtype=jnp.int32) < far_count[0], far_rows[0], -1
    )
    coupling_rows = couplings[0].transpose(1, 0, 2).reshape(rank, far_slots * rank)
    own_basis = lax.dynamic_slice_in_dim(row_basis, col * owned, owned, 0)
    own_basis = jnp.tile(own_basis.transpose(0, 2, 1), (1, 1, 3))
    far_source = far_cols[0]

    chips = col_count // 2
    chip, core = col // 2, col % 2
    each = jnp.arange(owned, dtype=jnp.int32)

    def clusters(chip_step, which):
        return (((chip + chip_step) % chips) * 2 + which) * owned + each

    def order(*chip_steps):
        return jnp.concatenate(
            [clusters(step, 1 - core) for step in chip_steps]
            + [clusters(step, core) for step in chip_steps]
        )

    far_chip = (far_target // (2 * owned) - chip) % chips
    far_core = (far_target // owned + 1 - core) % 2
    far_place = (far_core * chips + far_chip) * owned + far_target % owned
    far_place = jnp.where(far_target >= 0, far_place, -1)
    slot_rows = jnp.repeat(far_place, rank)[None, :]

    blocks = near_blocks[0]
    everyone = jnp.arange(targets, dtype=jnp.int32)
    middle = list(range(reach * owned, (reach + 1) * owned))
    inner = [column for column in range(owned, window - owned) if column not in middle]
    outer = list(range(owned)) + list(range(window - owned, window))
    (partial,) = near_terms(place, everyone, blocks, [slab], middle, [targets], window)
    below, above, partial, coupling_rows, slot_rows, far_source, own_basis = (
        lax.optimization_barrier(
            (below, above, partial, coupling_rows, slot_rows, far_source, own_basis)
        )
    )
    below_more = row_shift(below, 1)
    above_more = row_shift(above, -1)
    (partial,) = near_terms(
        place, everyone, blocks, [below, above], inner, [targets], window, partial
    )

    def rest(*chip_steps, far=None):
        return near_terms(
            place,
            order(*chip_steps),
            blocks,
            [below_more, above_more],
            outer,
            [owned * len(chip_steps)] + [owned] * len(chip_steps),
            window,
            partial,
            far,
        )

    moments, partial, below_more, above_more = lax.optimization_barrier(
        (moments, partial, below_more, above_more)
    )
    all_moments = lax.all_to_all(
        jnp.tile(moments, (row_count, 1)), "row", split_axis=0, concat_axis=0, tiled=True
    )
    sent, kept = rest(2)
    sent, all_moments = lax.optimization_barrier((sent, all_moments))
    got = other_core(sent)
    opposite = [add(kept[index], got[index]) for index in range(owned)]
    opposite, place = lax.optimization_barrier((opposite, place))
    from_below = chip_shift(opposite[0], 1)
    from_above = chip_shift(opposite[1], -1)
    sent, kept_up, kept_down, kept_far = rest(
        1, -1, far=(far_source, [all_moments], coupling_rows, slot_rows)
    )
    sent, from_below, from_above = lax.optimization_barrier((sent, from_below, from_above))
    got = other_core(sent)
    far = add(kept_far[0], got[2 * owned]).reshape(chips, owned * rank, excitations)
    early = [
        jnp.concatenate([add(kept_up[1], got[1]), far[1], far[2, :rank]]),
        jnp.concatenate([add(kept_down[0], got[owned]), far[chips - 1], far[2, rank:]]),
    ]
    early, place, own_far = lax.optimization_barrier((early, place, far[0]))
    early = [chip_shift(early[0], 1), chip_shift(early[1], -1)]
    sent, kept = rest(0)
    sent, early = lax.optimization_barrier((sent, early))
    passed = [side[leaf + owned * rank :] for side in early]
    late = [
        jnp.concatenate([add(kept_up[0], got[0], from_below), passed[0]]),
        jnp.concatenate([add(kept_down[1], got[owned + 1], from_above), passed[1]]),
    ]
    late = [chip_shift(late[0], 1), chip_shift(late[1], -1)]
    got = other_core(sent)
    return finish(kept, got, late, early, own_far, own_basis).reshape(panels, excitations)


def solution(mesh):
    placed = (
        P(("row", "col"), None),
        P(("row", "col"), None),
        P(("row", "col"), None),
        P(("row", "col"), None),
        P(("row", "col")),
        P(("row", "col"), None, None, None),
        P(("row", "col"), None),
        P(("row", "col"), None),
        P(("row", "col")),
        P(("row", "col"), None, None, None),
        P("row", None, None),
        P(("row", "col"), None, None),
    )
    return jax.shard_map(
        shards, mesh=mesh, in_specs=placed, out_specs=P(("row", "col"), None), check_vma=False
    )
```

```python
import jax
import jax.numpy as jnp
from jax import lax
from jax.experimental import pallas as pl
from jax.experimental.pallas import tpu as pltpu
from jax.sharding import PartitionSpec as P

reach = 2
across = 4


def in_hbm(*values):
    return [pltpu.with_memory_space_constraint(value, pltpu.HBM) for value in values]


def far_incoming(cols_ref, moments, coupling_ref, rows_ref, gathered, spread, arrived):
    slots = cols_ref.shape[0]
    rank = coupling_ref.shape[0]
    couplings = coupling_ref[...]
    rows = rows_ref[...]
    for target in range(spread.shape[0] // rank):
        spread[target * rank : (target + 1) * rank, :] = jnp.where(
            rows == target, couplings, jnp.zeros_like(couplings)
        )
    arrived()

    def pick(slot, carry):
        source = pl.multiple_of(cols_ref[slot] * rank, rank)
        here = pl.multiple_of(slot * rank, rank)
        gathered[pl.ds(here, rank), :] = moments[pl.ds(source, rank), :]
        return carry

    lax.fori_loop(0, slots, pick, 0, unroll=4)
    return jnp.dot(spread[...], gathered[...], preferred_element_type=jnp.float32)


def near_terms(place, targets, blocks, parts, columns, splits, window, partial=None, far=None):
    count = targets.shape[0]
    size = blocks.shape[1]
    part_rows, excitations = parts[0].shape
    per_target = len(columns)
    depth = per_target * size
    ahead = min(4, count)
    finishing = partial is not None
    far_cols, moment_parts, *coupling = far or (None, [])
    moment_sizes = [part.shape[0] for part in moment_parts]
    starts = [sum(splits[:index]) for index in range(len(splits))]

    def kernel(place_ref, target_ref, *rest):
        rest = list(rest)
        if far:
            cols_ref = rest.pop(0)
        blocks_ref = rest.pop(0)
        part_refs = [rest.pop(0) for _ in parts]
        if finishing:
            partial_ref = rest.pop(0)
        if far:
            moment_refs = [rest.pop(0) for _ in moment_parts]
            coupling_ref, rows_ref = rest.pop(0), rest.pop(0)
        out_refs = [rest.pop(0) for _ in splits]
        if far:
            far_ref = rest.pop(0)
        held, sources, result, held_sem, source_sem, result_sem = [rest.pop(0) for _ in range(6)]
        if finishing:
            running, running_sem = rest.pop(0), rest.pop(0)
        if far:
            moments, gathered, spread, moment_sem = rest

        def source_copy(index):
            return pltpu.make_async_copy(
                part_refs[index],
                sources.at[pl.ds(index * part_rows, part_rows), :],
                source_sem.at[index],
            )

        def running_copy(step):
            return pltpu.make_async_copy(
                partial_ref.at[target_ref[step]], running.at[step], running_sem.at[step]
            )

        def moment_copy(index):
            here = pl.ds(sum(moment_sizes[:index]), moment_sizes[index])
            return pltpu.make_async_copy(
                moment_refs[index], moments.at[here, :], moment_sem.at[index]
            )

        def far_copies():
            return (
                pltpu.make_async_copy(
                    result.at[count], out_refs[0].at[splits[0]], result_sem.at[count]
                ),
                pltpu.make_async_copy(
                    result.at[count + 1], far_ref.at[0], result_sem.at[count + 1]
                ),
            )

        def moments_arrived():
            for index in range(len(moment_parts)):
                moment_copy(index).wait()

        def begin(step):
            first = target_ref[step] * window
            for index, column in enumerate(columns):
                slot = jnp.maximum(place_ref[first + column], 0)
                pltpu.make_async_copy(
                    blocks_ref.at[slot], held.at[step * per_target + index], held_sem.at[step]
                ).start()
            if finishing:
                running_copy(step).start()

        def work(step):
            first = target_ref[step] * window
            pltpu.make_async_copy(
                blocks_ref.at[pl.ds(0, per_target)],
                held.at[pl.ds(step * per_target, per_target)],
                held_sem.at[step],
            ).wait()
            if finishing:
                running_copy(step).wait()
            total = None
            for index, column in enumerate(columns):
                here = jnp.where(
                    place_ref[first + column] >= 0, step * per_target + index, count * per_target
                )
                product = jnp.dot(
                    held[here],
                    sources[index * size : (index + 1) * size, :],
                    preferred_element_type=jnp.float32,
                )
                total = product if total is None else total + product
            if finishing:
                total = total + running[step].astype(jnp.float32)
            result[step] = total.astype(result.dtype)

        begin(0)
        for index in range(len(parts)):
            source_copy(index).start()
        for index in range(len(moment_parts)):
            moment_copy(index).start()
        for step in range(1, ahead):
            begin(step)
        held[count * per_target] = jnp.zeros((size, size), held.dtype)
        if far:
            incoming = far_incoming(
                cols_ref, moments, coupling_ref, rows_ref, gathered, spread, moments_arrived
            )
            result[count] = incoming[:size].astype(result.dtype)
            result[count + 1] = incoming[size:].astype(result.dtype)
            for copy in far_copies():
                copy.start()
        for index in range(len(parts)):
            source_copy(index).wait()

        def result_copy(index, step):
            return pltpu.make_async_copy(
                result.at[step], out_refs[index].at[step - starts[index]], result_sem.at[step]
            )

        for index in range(len(splits)):
            first, last = starts[index], starts[index] + splits[index]

            def both(step, carry):
                begin(step + ahead)
                return only(step, carry)

            def only(step, carry):
                work(step)
                result_copy(index, step).start()
                return carry

            middle = min(max(first, count - ahead), last)
            lax.fori_loop(first, middle, both, 0)
            lax.fori_loop(middle, last, only, 0)
        for index in range(len(splits)):

            def end(step, carry):
                result_copy(index, step).wait()
                return carry

            lax.fori_loop(starts[index], starts[index] + splits[index], end, 0)
        if far:
            for copy in far_copies():
                copy.wait()

    anywhere = pl.BlockSpec(memory_space=pltpu.HBM)
    extras = (partial,) if finishing else ()
    more = 2 if far else 0
    scratch = [
        pltpu.VMEM((count * per_target + 1, size, size), jnp.bfloat16),
        pltpu.VMEM((depth, excitations), jnp.bfloat16),
        pltpu.VMEM((count + more, size, excitations), jnp.bfloat16),
        pltpu.SemaphoreType.DMA((count,)),
        pltpu.SemaphoreType.DMA((len(parts),)),
        pltpu.SemaphoreType.DMA((count + more,)),
    ]
    if finishing:
        scratch += [
            pltpu.VMEM((count, size, excitations), jnp.bfloat16),
            pltpu.SemaphoreType.DMA((count,)),
        ]
    shapes = [(split, size, excitations) for split in splits]
    coupling_specs = [pl.BlockSpec(item.shape, lambda i, *_: (0, 0)) for item in coupling]
    if far:
        shapes[0] = (splits[0] + 1, size, excitations)
        shapes.append((1, size, excitations))
        scratch += [
            pltpu.VMEM((sum(moment_sizes), excitations), jnp.bfloat16),
            pltpu.VMEM((coupling[0].shape[1], excitations), jnp.bfloat16),
            pltpu.VMEM((2 * size, coupling[0].shape[1]), jnp.bfloat16),
            pltpu.SemaphoreType.DMA((len(moment_parts),)),
        ]
    return pl.pallas_call(
        kernel,
        grid_spec=pltpu.PrefetchScalarGridSpec(
            num_scalar_prefetch=3 if far else 2,
            grid=(1,),
            in_specs=[anywhere] * (1 + len(parts) + len(extras) + len(moment_parts))
            + coupling_specs,
            out_specs=[anywhere] * len(shapes),
            scratch_shapes=scratch,
        ),
        out_shape=[pltpu.HBM(shape, jnp.bfloat16) for shape in shapes],
        compiler_params=pltpu.CompilerParams(
            vmem_limit_bytes=2 * size * (count * per_target * size + (depth + 2 * count * size) * 2)
            + (14 if far else 4) * 2**20
        ),
        cost_estimate=pl.CostEstimate(
            flops=2 * count * size * depth * excitations,
            bytes_accessed=2 * (count * size * depth + depth * excitations),
            transcendentals=0,
        ),
        name="near_rest" if finishing else "near_first",
    )(
        place,
        targets,
        *([far_cols] if far else []),
        *in_hbm(blocks),
        *parts,
        *in_hbm(*extras),
        *moment_parts,
        *coupling,
    )


def finish_kernel(
    kept_ref, got_ref, below_late, above_late, below_early, above_early, far_ref, basis_ref, out_ref
):
    owned, size, _ = out_ref.shape
    rank = basis_ref.shape[2] // 3
    sides = [[below_late, above_early], [below_early, above_late]]
    relayed = [below_late, above_late]
    for cluster in range(owned):
        rows = slice(size + cluster * rank, size + (cluster + 1) * rank)
        incoming = far_ref[cluster * rank : (cluster + 1) * rank, :].astype(jnp.float32)
        incoming = incoming + below_early[rows, :].astype(jnp.float32)
        incoming = incoming + above_early[rows, :].astype(jnp.float32)
        incoming = incoming + relayed[cluster][size : size + rank, :].astype(jnp.float32)
        high = incoming.astype(jnp.bfloat16)
        left = incoming - high.astype(jnp.float32)
        middle = left.astype(jnp.bfloat16)
        low = (left - middle.astype(jnp.float32)).astype(jnp.bfloat16)
        total = jnp.dot(
            basis_ref[cluster],
            jnp.concatenate([high, middle, low]),
            preferred_element_type=jnp.float32,
        )
        total = total + kept_ref[cluster].astype(jnp.float32)
        total = total + got_ref[cluster].astype(jnp.float32)
        for side in sides[cluster]:
            total = total + side[0:size, :].astype(jnp.float32)
        out_ref[cluster] = total.astype(out_ref.dtype)


def finish(kept, got, late, early, far, basis):
    operands = [kept, got, *late, *early, far, basis]
    whole = pl.BlockSpec(memory_space=pltpu.VMEM)
    return pl.pallas_call(
        finish_kernel,
        in_specs=[whole] * len(operands),
        out_specs=whole,
        out_shape=jax.ShapeDtypeStruct(kept.shape, jnp.bfloat16),
        compiler_params=pltpu.CompilerParams(vmem_limit_bytes=16 * 2**20),
        cost_estimate=pl.CostEstimate(
            flops=2 * kept.size * basis.shape[2],
            bytes_accessed=2 * 5 * kept.size,
            transcendentals=0,
        ),
        name="finish",
    )(*operands)


def add(*terms):
    total = terms[0].astype(jnp.float32)
    for term in terms[1:]:
        total = total + term.astype(jnp.float32)
    return total.astype(jnp.bfloat16)


def shards(
    charges,
    send_order,
    near_rows,
    near_cols,
    near_count,
    near_blocks,
    far_rows,
    far_cols,
    far_count,
    couplings,
    row_basis,
    col_basis,
):
    row_count = lax.axis_size("row")
    col_count = lax.axis_size("col")
    device_count = row_count * col_count
    panels, excitations = charges.shape
    segment = panels // device_count
    owned, rank, leaf = col_basis.shape
    targets = row_basis.shape[0]
    window = (2 * reach + 1) * owned
    row = lax.axis_index("row")
    col = lax.axis_index("col")

    outgoing = charges.at[send_order[0]].get(mode="promise_in_bounds")
    incoming = lax.all_to_all(
        outgoing.reshape(device_count, segment, excitations),
        ("row", "col"),
        split_axis=0,
        concat_axis=0,
        tiled=True,
    )
    slab = incoming.reshape(panels, excitations)
    (
        slab,
        near_rows,
        near_cols,
        near_count,
        far_rows,
        far_cols,
        far_count,
        couplings,
        row_basis,
    ) = lax.optimization_barrier(
        (
            slab,
            near_rows,
            near_cols,
            near_count,
            far_rows,
            far_cols,
            far_count,
            couplings,
            row_basis,
        )
    )
    def row_shift(value, step):
        return lax.ppermute(value, "row", [(i, (i + step) % row_count) for i in range(row_count)])

    def line_shift(value, step):
        return lax.ppermute(
            value,
            "row",
            [(i, i // across * across + (i + step) % across) for i in range(row_count)],
        )

    def other_core(value):
        return lax.ppermute(value, "col", [(i, i ^ 1) for i in range(col_count)])

    def chip_shift(value, step):
        return lax.ppermute(
            value, "col", [(i, (i + 2 * step) % col_count) for i in range(col_count)]
        )

    below = row_shift(slab, 1)
    above = row_shift(slab, -1)
    slots = jnp.arange(near_rows.shape[1], dtype=jnp.int32)
    pair = near_rows[0] * window + near_cols[0] - (row - reach) * owned
    pair = jnp.where(slots < near_count[0], pair, -1)
    wanted = jnp.arange(targets * window, dtype=jnp.int32)
    place = jnp.max(jnp.where(pair[None, :] == wanted[:, None], slots[None, :], -1), axis=1)

    far_slots = far_rows.shape[1]
    far_target = jnp.where(
        jnp.arange(far_slots, dtype=jnp.int32) < far_count[0], far_rows[0], -1
    )
    coupling_rows = couplings[0].transpose(1, 0, 2).reshape(rank, far_slots * rank)
    own_basis = lax.dynamic_slice_in_dim(row_basis, col * owned, owned, 0)
    own_basis = jnp.tile(own_basis.transpose(0, 2, 1), (1, 1, 3))
    far_row = far_cols[0] // owned
    far_line = (far_row // across - row // across) % (row_count // across)
    far_place = (far_row - row) % across
    far_source = (far_line * across + far_place) * owned + far_cols[0] % owned

    chips = col_count // 2
    chip, core = col // 2, col % 2
    each = jnp.arange(owned, dtype=jnp.int32)

    def clusters(chip_step, which):
        return (((chip + chip_step) % chips) * 2 + which) * owned + each

    def order(*chip_steps):
        return jnp.concatenate(
            [clusters(step, 1 - core) for step in chip_steps]
            + [clusters(step, core) for step in chip_steps]
        )

    far_chip = (far_target // (2 * owned) - chip) % chips
    far_core = (far_target // owned + 1 - core) % 2
    far_place = (far_core * chips + far_chip) * owned + far_target % owned
    far_place = jnp.where(far_target >= 0, far_place, -1)
    slot_rows = jnp.repeat(far_place, rank)[None, :]

    blocks = near_blocks[0]
    everyone = jnp.arange(targets, dtype=jnp.int32)
    middle = list(range(reach * owned, (reach + 1) * owned))
    inner = [column for column in range(owned, window - owned) if column not in middle]
    outer = list(range(owned)) + list(range(window - owned, window))
    (partial,) = near_terms(place, everyone, blocks, [slab], middle, [targets], window)
    slab, partial = lax.optimization_barrier((slab, partial))
    moments = (
        jnp.einsum(
            "gkb,gbr->gkr",
            col_basis,
            slab.reshape(owned, leaf, excitations),
            preferred_element_type=jnp.float32,
        )
        .astype(jnp.bfloat16)
        .reshape(owned * rank, excitations)
    )
    of_line = [moments] + [line_shift(moments, -step) for step in range(1, across)]
    below, above, partial, of_line, coupling_rows, slot_rows, far_source, own_basis = (
        lax.optimization_barrier(
            (below, above, partial, of_line, coupling_rows, slot_rows, far_source, own_basis)
        )
    )
    below_more = row_shift(below, 1)
    above_more = row_shift(above, -1)
    (partial,) = near_terms(
        place, everyone, blocks, [below, above], inner, [targets], window, partial
    )

    def rest(*chip_steps, far=None):
        return near_terms(
            place,
            order(*chip_steps),
            blocks,
            [below_more, above_more],
            outer,
            [owned * len(chip_steps)] + [owned] * len(chip_steps),
            window,
            partial,
            far,
        )

    of_line, partial = lax.optimization_barrier((jnp.concatenate(of_line), partial))
    next_line = row_shift(of_line, -across)
    last_line = row_shift(of_line, across)
    sent, kept = rest(2)
    sent, next_line, last_line = lax.optimization_barrier((sent, next_line, last_line))
    half = of_line.shape[0] // 2
    second_line = [row_shift(next_line[:half], -across), row_shift(last_line[half:], across)]
    got = other_core(sent)
    opposite = [add(kept[index], got[index]) for index in range(owned)]
    opposite, place, second_line = lax.optimization_barrier((opposite, place, second_line))
    from_below = chip_shift(opposite[0], 1)
    from_above = chip_shift(opposite[1], -1)
    moment_parts = [of_line, next_line, *second_line, last_line]
    sent, kept_up, kept_down, kept_far = rest(
        1, -1, far=(far_source, moment_parts, coupling_rows, slot_rows)
    )
    sent, from_below, from_above = lax.optimization_barrier((sent, from_below, from_above))
    got = other_core(sent)
    far = add(kept_far[0], got[2 * owned]).reshape(chips, owned * rank, excitations)
    early = [
        jnp.concatenate([add(kept_up[1], got[1]), far[1], far[2, :rank]]),
        jnp.concatenate([add(kept_down[0], got[owned]), far[chips - 1], far[2, rank:]]),
    ]
    early, place, own_far = lax.optimization_barrier((early, place, far[0]))
    early = [chip_shift(early[0], 1), chip_shift(early[1], -1)]
    sent, kept = rest(0)
    sent, early = lax.optimization_barrier((sent, early))
    passed = [side[leaf + owned * rank :] for side in early]
    late = [
        jnp.concatenate([add(kept_up[0], got[0], from_below), passed[0]]),
        jnp.concatenate([add(kept_down[1], got[owned + 1], from_above), passed[1]]),
    ]
    late = [chip_shift(late[0], 1), chip_shift(late[1], -1)]
    got = other_core(sent)
    return finish(kept, got, late, early, own_far, own_basis).reshape(panels, excitations)


def solution(mesh):
    placed = (
        P(("row", "col"), None),
        P(("row", "col"), None),
        P(("row", "col"), None),
        P(("row", "col"), None),
        P(("row", "col")),
        P(("row", "col"), None, None, None),
        P(("row", "col"), None),
        P(("row", "col"), None),
        P(("row", "col")),
        P(("row", "col"), None, None, None),
        P("row", None, None),
        P(("row", "col"), None, None),
    )
    return jax.shard_map(
        shards, mesh=mesh, in_specs=placed, out_specs=P(("row", "col"), None), check_vma=False
    )
```
